128 devices in a mesh: tile: 32 (over z, x, core), group: 4 (over y).
Axes of the slice: x: 4, y: 4, z: 4, core: 2. Of those that a mesh axis runs over, the one named last changes fastest.
Arguments:
- latent: bfloat16 [8, 256, 40, 384], P('group', 'tile'), may hold values from -6 to 6
- conv_first: bfloat16 [3, 3, 3, 384, 384], replicated, may hold values from -0.0625 to 0.0625
- conv_second: bfloat16 [3, 3, 3, 384, 384], replicated, may hold values from -0.0625 to 0.0625
- time_weight: bfloat16 [3, 384, 768], replicated, may hold values from -0.1875 to 0.1875
- space_weight: bfloat16 [3, 3, 384, 192], replicated, may hold values from -0.109375 to 0.109375
Outputs:
- decoded: bfloat16 [16, 512, 80, 192], P('group', 'tile')
The draws below stay inside these ranges and needn't reach their ends.
All inputs are finite; a program needn't handle non-finite values.
Results may differ from the reference program's by a relative error of at most 0.0085.
Values may be sent and summed in bfloat16 or wider, within the bound.
A program may use at most 128 MiB of HBM per device.

```python
import jax
import jax.numpy as jnp
from jax import lax

C = 384
CO = 192
W = 40
FRAMES = 8
ROWS = 256


def level_of(key, extent, cuts, low, top_value):
    def one(dim, blocks):
        heights = jax.random.uniform(jax.random.fold_in(jax.random.fold_in(key, 6), dim), (blocks,), jnp.float32, low / len(cuts), top_value / len(cuts))
        return jnp.repeat(jnp.exp(heights), extent[dim] // blocks).reshape((-1,) + (1,) * (len(extent) - dim - 1))

    level = one(*cuts[0])
    for cut in cuts[1:]:
        level = level * one(*cut)
    return level


def gaussian(own_key, dims, scale, most, cuts=(), kind=jnp.bfloat16):
    loudness = level_of(own_key, dims, cuts, -0.22, 0.18) if cuts else 1.0
    drawn = jax.random.normal(own_key, dims, jnp.float32) * scale * loudness
    return jnp.minimum(jnp.maximum(drawn, -most), most).astype(kind)


def setup_inputs(seed: int = 0) -> dict:
    splits = jax.random.split(jax.random.key(seed), 6)
    return {
        "latent": gaussian(splits[0], (FRAMES, ROWS, W, C), 1.0, 6.0, ((0, 4), (1, 32))),
        "conv_first": gaussian(splits[1], (3, 3, 3, C, C), (27 * C) ** -0.5, 0.0625),
        "conv_second": gaussian(splits[2], (3, 3, 3, C, C), (27 * C) ** -0.5, 0.0625),
        "time_weight": gaussian(splits[3], (3, C, 2 * C), (3 * C) ** -0.5, 0.1875),
        "space_weight": gaussian(splits[4], (3, 3, C, CO), (9 * C) ** -0.5, 0.109375),
    }


def rms_silu(value):
    value = value.astype(jnp.float32)
    value = value * lax.rsqrt(lax.optimization_barrier(jnp.mean(value * value, axis=-1, keepdims=True)) + 1e-06)
    return jax.nn.silu(value).astype(jnp.bfloat16)

def conv_cube(padded, weight):
    frames = padded.shape[0] - 2
    rows = padded.shape[1] - 2
    width = padded.shape[2]
    chans = padded.shape[3]
    outs = weight.shape[4]
    cols = jnp.pad(padded, ((0, 0), (0, 0), (1, 1), (0, 0)))
    wide = jnp.concatenate([cols[:, :, k:k + width] for k in range(3)], axis=-1)
    folded = weight.reshape(3, 3, 3 * chans, outs)
    total = jnp.zeros((frames * rows * width, outs), jnp.float32)
    for a in range(3):
        for b in range(3):
            piece = wide[a:a + frames, b:b + rows].reshape(-1, 3 * chans)
            total = total + jnp.dot(piece, folded[a, b], preferred_element_type=jnp.float32)
    return total.reshape(frames, rows, width, outs)

def time_double(padded, weight):
    frames = padded.shape[0] - 2
    rows, width, chans = (padded.shape[1], padded.shape[2], padded.shape[3])
    total = jnp.zeros((frames * rows * width, 2 * chans), jnp.float32)
    for a in range(3):
        total = total + jnp.dot(padded[a:a + frames].reshape(-1, chans), weight[a], preferred_element_type=jnp.float32)
    split = total.reshape(frames, rows, width, 2, chans)
    split = jnp.transpose(split, (0, 3, 1, 2, 4))
    return split.reshape(2 * frames, rows, width, chans).astype(jnp.bfloat16)

def space_conv(rows_ext, weight):
    rows = rows_ext.shape[1] - 2
    chans = rows_ext.shape[3]
    outs = weight.shape[3]
    upper = jnp.repeat(rows_ext, 2, axis=1)[:, 1:-1]
    upper = jnp.repeat(upper, 2, axis=2)
    width = upper.shape[2]
    cols = jnp.pad(upper, ((0, 0), (0, 0), (1, 1), (0, 0)))
    wide = jnp.concatenate([cols[:, :, k:k + width] for k in range(3)], axis=-1)
    folded = weight.reshape(3, 3 * chans, outs)
    count = upper.shape[0]
    total = jnp.zeros((count * 2 * rows * width, outs), jnp.float32)
    for b in range(3):
        total = total + jnp.dot(wide[:, b:b + 2 * rows].reshape(-1, 3 * chans), folded[b], preferred_element_type=jnp.float32)
    return total.reshape(count, 2 * rows, width, outs).astype(jnp.bfloat16)

def reference(latent, conv_first, conv_second, time_weight, space_weight):
    first = rms_silu(latent)
    padded = jnp.pad(first, ((2, 0), (1, 1), (0, 0), (0, 0)))
    second = rms_silu(conv_cube(padded, conv_first))
    padded = jnp.pad(second, ((2, 0), (1, 1), (0, 0), (0, 0)))
    mixed = (latent.astype(jnp.float32) + conv_cube(padded, conv_second)).astype(jnp.bfloat16)
    upframes = time_double(jnp.pad(mixed, ((2, 0), (0, 0), (0, 0), (0, 0))), time_weight)
    rows_ext = jnp.pad(upframes, ((0, 0), (1, 1), (0, 0), (0, 0)))
    decoded = lax.map(lambda frame: space_conv(frame[None], space_weight)[0], rows_ext)
    return decoded
```

```python
import functools

import jax
import jax.numpy as jnp
from jax import lax
from jax.experimental import pallas as pl
from jax.experimental.pallas import tpu as pltpu
from jax.sharding import PartitionSpec as P

MESH = pl.DeviceIdType.MESH
BF = jnp.bfloat16
F32 = jnp.float32

OUTER = ((0, 2), (6, 2))
INNER = ((2, 4),)
OUTER_SENDS = ((1, 1), (8, 1), (2, 1), (7, 1))
INNER_SENDS = ((3, 1), (6, 1), (4, 2))
SENDS = OUTER_SENDS + INNER_SENDS
NY = len(SENDS)


def rms_silu(v):
    v = v * lax.rsqrt(jnp.mean(v * v, axis=-1, keepdims=True) + 1e-06)
    return v / (1.0 + jnp.exp(-v))


def shift_down(v):
    at = lax.broadcasted_iota(jnp.int32, v.shape, 0)
    return jnp.where(at == 0, 0.0, pltpu.roll(v, 1, 0))


def shift_up(v):
    at = lax.broadcasted_iota(jnp.int32, v.shape, 0)
    return jnp.where(at == v.shape[0] - 1, 0.0, pltpu.roll(v, v.shape[0] - 1, 0))


def kernel(
    tiles, groups,
    latent, conv_first, conv_second, time_weight, space_weight, out,
    lat, X, W, wt, ws, wsp, Y, U, Z, T, O,
    lat_sem, w_sem, wt_sem, ws_sem, out_sem, y_send, y_recv, t_send, t_recv,
):
    t = lax.axis_index("tile")
    g = lax.axis_index("group")
    wide = lat.shape[2]
    ch = lat.shape[3]
    has_up, has_down = t > 0, t < tiles - 1
    has_prev, has_next = g > 0, g < groups - 1
    up = (lax.rem(t + tiles - 1, tiles), g)
    down = (lax.rem(t + 1, tiles), g)
    prev = (t, lax.rem(g + groups - 1, groups))
    after = (t, lax.rem(g + 1, groups))

    barrier = pltpu.get_barrier_semaphore()
    for other in (up, down, prev, after):
        pl.semaphore_signal(barrier, inc=1, device_id=other, device_id_type=MESH)

    lat_copy = pltpu.make_async_copy(latent, lat, lat_sem)
    lat_copy.start()
    w_copies = []
    for s, src in ((0, conv_first), (1, conv_second)):
        for a in (2, 1, 0):
            for b in range(3):
                w_copies.append(pltpu.make_async_copy(src.at[a, b], W.at[s, a, b], w_sem.at[s, a, b]))
    for c in w_copies[:9]:
        c.start()
    wt_copy = pltpu.make_async_copy(time_weight, wt, wt_sem)
    ws_copy = pltpu.make_async_copy(space_weight, ws, ws_sem)
    ws_copy.start()
    for c in w_copies[9:]:
        c.start()
    wt_copy.start()

    def wait_w(s, a):
        for b in range(3):
            pltpu.make_async_copy(conv_first.at[a, b], W.at[s, a, b], w_sem.at[s, a, b]).wait()

    @pl.when(jnp.logical_not(has_prev))
    def _():
        for s in range(3):
            for f in range(2):
                X[s, f] = jnp.zeros(X.shape[2:], BF)

    @pl.when(jnp.logical_not(has_up))
    def _():
        for s in range(3):
            X[s, :, 0] = jnp.zeros((4,) + X.shape[3:], BF)

    @pl.when(jnp.logical_not(has_down))
    def _():
        for s in range(3):
            X[s, :, 9] = jnp.zeros((4,) + X.shape[3:], BF)

    lat_copy.wait()

    def act_own(i, c):
        f, r = i // 8, i % 8
        X[0, 2 + f, 1 + r] = rms_silu(lat[f, r].astype(F32)).astype(BF)
        return c

    lax.fori_loop(0, 16, act_own, 0)

    pl.semaphore_wait(barrier, 4)

    def y_copy(s, k):
        row, count = SENDS[k]
        return pltpu.make_async_remote_copy(
            src_ref=X.at[s, pl.ds(2, 2), pl.ds(row, count)],
            dst_ref=X.at[s, pl.ds(0, 2), pl.ds(row, count)],
            send_sem=y_send.at[s, k],
            recv_sem=y_recv.at[s, k],
            device_id=after,
            device_id_type=MESH,
        )

    def t_copy(s, k):
        frame = 2 if k < 2 else 0
        row, slot, other = (1, 9, up) if k % 2 == 0 else (8, 0, down)
        return pltpu.make_async_remote_copy(
            src_ref=X.at[s, pl.ds(frame, 2), row],
            dst_ref=X.at[s, pl.ds(frame, 2), slot],
            send_sem=t_send.at[s, k],
            recv_sem=t_recv.at[s, k],
            device_id=other,
            device_id_type=MESH,
        )

    def send_outer(s):
        @pl.when(has_next)
        def _():
            y_copy(s, 0).start()
            y_copy(s, 1).start()

        @pl.when(has_up)
        def _():
            t_copy(s, 0).start()

        @pl.when(has_down)
        def _():
            t_copy(s, 1).start()

        @pl.when(has_next)
        def _():
            y_copy(s, 2).start()
            y_copy(s, 3).start()

    def send_inner(s):
        @pl.when(has_next)
        def _():
            for k in range(len(OUTER_SENDS), NY):
                y_copy(s, k).start()

    def wait_own_halo(s):
        @pl.when(has_down)
        def _():
            t_copy(s, 0).wait_recv()

        @pl.when(has_up)
        def _():
            t_copy(s, 1).wait_recv()

    def forward(s):
        @pl.when(has_prev)
        def _():
            y_copy(s, 0).wait_recv()

            @pl.when(has_up)
            def _():
                t_copy(s, 2).start()

            y_copy(s, 1).wait_recv()

            @pl.when(has_down)
            def _():
                t_copy(s, 3).start()

    def wait_outer(s):
        @pl.when(has_prev)
        def _():
            for k in range(2, NY - 1):
                y_copy(s, k).wait_recv()

            @pl.when(has_down)
            def _():
                t_copy(s, 2).wait_recv()

            @pl.when(has_up)
            def _():
                t_copy(s, 3).wait_recv()

    def wait_inner(s):
        @pl.when(has_prev)
        def _():
            y_copy(s, NY - 1).wait_recv()

    def taps(s, a, frames, spans, first):
        parts = []
        for b in range(3):
            rows = []
            for f in frames:
                for r, n in spans:
                    rows.append(X[s, f + a, r + b : r + b + n].reshape(n * wide, ch))
            parts.append(jnp.concatenate(rows, axis=0))
        lhs = jnp.concatenate(parts, axis=1)
        rhs = jnp.concatenate(
            [jnp.concatenate([W[s, a, b, e] for e in range(3)], axis=1) for b in range(3)], axis=0
        )
        d = jnp.dot(lhs, rhs, preferred_element_type=F32)
        at = 0
        for f in frames:
            for r, n in spans:
                piece = d[at : at + n * wide].reshape(n, wide, 3 * ch)
                if first:
                    Y[f, r : r + n] = piece
                else:
                    Y[f, r : r + n] += piece
                at += n * wide

    def own(s, spans):
        taps(s, 2, (0, 1), spans, True)
        taps(s, 1, (1,), spans, False)

    def earlier(s, spans):
        taps(s, 1, (0,), spans, False)
        taps(s, 0, (0, 1), spans, False)

    def total(f, r):
        y = Y[f, r]
        return shift_down(y[:, :ch]) + y[:, ch : 2 * ch] + shift_up(y[:, 2 * ch :])

    def finish(s, spread):
        def step(i, c):
            f, j = i // 4, i % 4
            r = j + (j // 2) * 4 if spread else j + 2
            v = total(f, r)
            if s == 0:
                v = rms_silu(v)
            else:
                v = lat[f, r].astype(F32) + v
            X[s + 1, 2 + f, 1 + r] = v.astype(BF)
            return c

        lax.fori_loop(0, 8, step, 0)

    send_outer(0)
    send_inner(0)

    ws_copy.wait()
    co = ws.shape[3]
    wsp[...] = jnp.zeros(wsp.shape, BF)
    for p, half, bs in ((0, 0, (0,)), (0, 1, (1, 2)), (1, 0, (0, 1)), (1, 1, (2,))):
        es = []
        for e in range(3):
            v = ws[bs[0], e].astype(F32)
            for b in bs[1:]:
                v = v + ws[b, e].astype(F32)
            es.append(v)
        rows = pl.ds(half * ch, ch)
        wsp[p, rows, 0:co] = (es[0] + es[1] + es[2]).astype(BF)
        wsp[p, rows, 256 : 256 + co] = es[0].astype(BF)
        wsp[p, rows, 512 : 512 + co] = es[2].astype(BF)

    for s in range(2):
        wait_w(s, 2)
        wait_w(s, 1)
        own(s, INNER)
        wait_own_halo(s)
        forward(s)
        own(s, OUTER)
        wait_w(s, 0)
        wait_outer(s)
        earlier(s, OUTER)
        finish(s, True)
        send_outer(s + 1)
        wait_inner(s)
        earlier(s, INNER)
        finish(s, False)
        send_inner(s + 1)

    wt_copy.wait()
    wait_own_halo(2)
    forward(2)

    def double(spans):
        parts = []
        for a in range(3):
            rows = []
            for f in range(2):
                for r, n in spans:
                    rows.append(X[2, f + a, r : r + n].reshape(n * wide, ch))
            parts.append(jnp.concatenate(rows, axis=0))
        lhs = jnp.concatenate(parts, axis=1)
        rhs = jnp.concatenate([wt[a] for a in range(3)], axis=0)
        d = jnp.dot(lhs, rhs, preferred_element_type=F32).astype(BF)
        at = 0
        for f in range(2):
            for r, n in spans:
                for j in range(2):
                    U[2 * f + j, r : r + n] = d[at : at + n * wide, j * ch : (j + 1) * ch].reshape(n, wide, ch)
                at += n * wide

    def space(spans, spread):
        for p in range(2):
            for f in range(4):
                parts = []
                for h in range(2):
                    rows = [U[f, r + p + h : r + p + h + n].reshape(n * wide, ch) for r, n in spans]
                    parts.append(jnp.concatenate(rows, axis=0))
                lhs = jnp.concatenate(parts, axis=1)
                d = jnp.dot(lhs, wsp[p], preferred_element_type=F32)
                Z[f] = d.reshape(4, wide, 768)

            def step(i, c):
                f, j = i // 4, i % 4
                r = j + (j // 2) * 4 if spread else j + 2
                z = Z[f, j]
                mid, left, right = z[:, :256], z[:, 256:512], z[:, 512:]
                even = mid - left + shift_down(left)
                odd = mid - right + shift_up(right)
                for h in range(2):
                    T[h, pl.ds(0, wide, stride=2), :] = even[:, h * 128 : (h + 1) * 128]
                    T[h, pl.ds(1, wide, stride=2), :] = odd[:, h * 128 : (h + 1) * 128]
                O[f, 2 * r + p, :, 0:128] = T[0].astype(BF)
                O[f, 2 * r + p, :, 128:co] = T[1, :, 0 : co - 128].astype(BF)
                return c

            lax.fori_loop(0, 16, step, 0)

    def out_copy(k):
        row, n = ((0, 4), (12, 4), (4, 8))[k]
        return pltpu.make_async_copy(
            O.at[:, pl.ds(row, n)], out.at[:, pl.ds(row, n)], out_sem.at[k]
        )

    wait_outer(2)
    double(((0, 4), (6, 4)))
    space(OUTER, True)
    out_copy(0).start()
    out_copy(1).start()
    wait_inner(2)
    double(((4, 2),))
    space(INNER, False)
    out_copy(2).start()

    for s in range(3):
        @pl.when(has_next)
        def _():
            for k in range(NY):
                y_copy(s, k).wait_send()

        @pl.when(has_up)
        def _():
            t_copy(s, 0).wait_send()

            @pl.when(has_prev)
            def _():
                t_copy(s, 2).wait_send()

        @pl.when(has_down)
        def _():
            t_copy(s, 1).wait_send()

            @pl.when(has_prev)
            def _():
                t_copy(s, 3).wait_send()

    for k in range(3):
        out_copy(k).wait()


def solution(mesh):
    tiles, groups = mesh.shape["tile"], mesh.shape["group"]

    def local(latent, conv_first, conv_second, time_weight, space_weight):
        frames, rows, wide, ch = latent.shape
        co = space_weight.shape[3]
        hbm = pl.BlockSpec(memory_space=pltpu.HBM)
        dma = pltpu.SemaphoreType.DMA
        return pl.pallas_call(
            functools.partial(kernel, tiles, groups),
            name="block",
            out_shape=jax.ShapeDtypeStruct((2 * frames, 2 * rows, 2 * wide, co), BF),
            in_specs=[hbm] * 5,
            out_specs=hbm,
            scratch_shapes=[
                pltpu.VMEM((2, 8, wide, ch), BF),
                pltpu.VMEM((3, 4, 10, wide, ch), BF),
                pltpu.VMEM((2, 3, 3, 3, ch, ch), BF),
                pltpu.VMEM((3, ch, 2 * ch), BF),
                pltpu.VMEM((3, 3, ch, co), BF),
                pltpu.VMEM((2, 2 * ch, 768), BF),
                pltpu.VMEM((2, 8, wide, 3 * ch), F32),
                pltpu.VMEM((4, 10, wide, ch), BF),
                pltpu.VMEM((4, 4, wide, 768), F32),
                pltpu.VMEM((2, 2 * wide, 128), F32),
                pltpu.VMEM((4, 16, 2 * wide, co), BF),
                dma,
                dma((2, 3, 3)),
                dma,
                dma,
                dma((3,)),
                dma((3, NY)),
                dma((3, NY)),
                dma((3, 4)),
                dma((3, 4)),
            ],
            compiler_params=pltpu.CompilerParams(
                collective_id=0, has_side_effects=True, vmem_limit_bytes=60 * 2**20
            ),
        )(latent, conv_first, conv_second, time_weight, space_weight)

    return jax.shard_map(
        local,
        mesh=mesh,
        in_specs=(P("group", "tile", None, None), P(), P(), P(), P()),
        out_specs=P("group", "tile", None, None),
        check_vma=False,
    )
```

```python
import functools

import jax
import jax.numpy as jnp
from jax import lax
from jax.experimental import pallas as pl
from jax.experimental.pallas import tpu as pltpu
from jax.sharding import PartitionSpec as P

MESH = pl.DeviceIdType.MESH
BF = jnp.bfloat16
F32 = jnp.float32

OUTER = ((0, 2), (6, 2))
INNER = ((2, 4),)
OUTER_SENDS = ((1, 1), (8, 1), (2, 1), (7, 1))
INNER_SENDS = ((3, 1), (6, 1), (4, 2))
SENDS = OUTER_SENDS + INNER_SENDS
NY = len(SENDS)


def rms_silu(v):
    v = v * lax.rsqrt(jnp.mean(v * v, axis=-1, keepdims=True) + 1e-06)
    return v / (1.0 + jnp.exp(-v))


def shift_down(v):
    at = lax.broadcasted_iota(jnp.int32, v.shape, 0)
    return jnp.where(at == 0, 0.0, pltpu.roll(v, 1, 0))


def shift_up(v):
    at = lax.broadcasted_iota(jnp.int32, v.shape, 0)
    return jnp.where(at == v.shape[0] - 1, 0.0, pltpu.roll(v, v.shape[0] - 1, 0))


def kernel(
    tiles, groups,
    latent, conv_first, conv_second, time_weight, space_weight, out,
    lat, X, W, wt, ws, wsp, Y, U, Z, T,
    lat_sem, w_sem, wt_sem, ws_sem, y_send, y_recv, t_send, t_recv,
):
    t = lax.axis_index("tile")
    g = lax.axis_index("group")
    wide = lat.shape[2]
    ch = lat.shape[3]
    has_up, has_down = t > 0, t < tiles - 1
    has_prev, has_next = g > 0, g < groups - 1
    up = (lax.rem(t + tiles - 1, tiles), g)
    down = (lax.rem(t + 1, tiles), g)
    prev = (t, lax.rem(g + groups - 1, groups))
    after = (t, lax.rem(g + 1, groups))

    barrier = pltpu.get_barrier_semaphore()
    for other in (up, down, prev, after):
        pl.semaphore_signal(barrier, inc=1, device_id=other, device_id_type=MESH)

    lat_copy = pltpu.make_async_copy(latent, lat, lat_sem)
    lat_copy.start()
    w_copies = []
    for s, src in ((0, conv_first), (1, conv_second)):
        for a in (2, 1, 0):
            for b in range(3):
                w_copies.append(pltpu.make_async_copy(src.at[a, b], W.at[s, a, b], w_sem.at[s, a, b]))
    for c in w_copies[:9]:
        c.start()
    wt_copy = pltpu.make_async_copy(time_weight, wt, wt_sem)
    ws_copy = pltpu.make_async_copy(space_weight, ws, ws_sem)
    ws_copy.start()
    for c in w_copies[9:]:
        c.start()
    wt_copy.start()

    def wait_w(s, a):
        for b in range(3):
            pltpu.make_async_copy(conv_first.at[a, b], W.at[s, a, b], w_sem.at[s, a, b]).wait()

    @pl.when(jnp.logical_not(has_prev))
    def _():
        for s in range(3):
            for f in range(2):
                X[s, f] = jnp.zeros(X.shape[2:], BF)

    @pl.when(jnp.logical_not(has_up))
    def _():
        for s in range(3):
            X[s, :, 0] = jnp.zeros((4,) + X.shape[3:], BF)

    @pl.when(jnp.logical_not(has_down))
    def _():
        for s in range(3):
            X[s, :, 9] = jnp.zeros((4,) + X.shape[3:], BF)

    lat_copy.wait()

    def act_own(i, c):
        f, r = i // 8, i % 8
        X[0, 2 + f, 1 + r] = rms_silu(lat[f, r].astype(F32)).astype(BF)
        return c

    lax.fori_loop(0, 16, act_own, 0, unroll=4)

    pl.semaphore_wait(barrier, 4)

    def y_copy(s, k):
        row, count = SENDS[k]
        return pltpu.make_async_remote_copy(
            src_ref=X.at[s, pl.ds(2, 2), pl.ds(row, count)],
            dst_ref=X.at[s, pl.ds(0, 2), pl.ds(row, count)],
            send_sem=y_send.at[s, k],
            recv_sem=y_recv.at[s, k],
            device_id=after,
            device_id_type=MESH,
        )

    def t_copy(s, k):
        frame = 2 if k < 2 else 0
        row, slot, other = (1, 9, up) if k % 2 == 0 else (8, 0, down)
        return pltpu.make_async_remote_copy(
            src_ref=X.at[s, pl.ds(frame, 2), row],
            dst_ref=X.at[s, pl.ds(frame, 2), slot],
            send_sem=t_send.at[s, k],
            recv_sem=t_recv.at[s, k],
            device_id=other,
            device_id_type=MESH,
        )

    def send_outer(s):
        @pl.when(has_next)
        def _():
            y_copy(s, 0).start()
            y_copy(s, 1).start()

        @pl.when(has_up)
        def _():
            t_copy(s, 0).start()

        @pl.when(has_down)
        def _():
            t_copy(s, 1).start()

        @pl.when(has_next)
        def _():
            y_copy(s, 2).start()
            y_copy(s, 3).start()

    def send_inner(s):
        @pl.when(has_next)
        def _():
            for k in range(len(OUTER_SENDS), NY):
                y_copy(s, k).start()

    def wait_own_halo(s):
        @pl.when(has_down)
        def _():
            t_copy(s, 0).wait_recv()

        @pl.when(has_up)
        def _():
            t_copy(s, 1).wait_recv()

    def forward(s):
        @pl.when(has_prev)
        def _():
            y_copy(s, 0).wait_recv()

            @pl.when(has_up)
            def _():
                t_copy(s, 2).start()

            y_copy(s, 1).wait_recv()

            @pl.when(has_down)
            def _():
                t_copy(s, 3).start()

    def wait_outer(s):
        @pl.when(has_prev)
        def _():
            for k in range(2, NY - 1):
                y_copy(s, k).wait_recv()

            @pl.when(has_down)
            def _():
                t_copy(s, 2).wait_recv()

            @pl.when(has_up)
            def _():
                t_copy(s, 3).wait_recv()

    def wait_inner(s):
        @pl.when(has_prev)
        def _():
            y_copy(s, NY - 1).wait_recv()

    def taps(s, a, frames, spans, first):
        parts = []
        for b in range(3):
            rows = []
            for f in frames:
                for r, n in spans:
                    rows.append(X[s, f + a, r + b : r + b + n].reshape(n * wide, ch))
            parts.append(jnp.concatenate(rows, axis=0))
        lhs = jnp.concatenate(parts, axis=1)
        rhs = jnp.concatenate(
            [jnp.concatenate([W[s, a, b, e] for e in range(3)], axis=1) for b in range(3)], axis=0
        )
        d = jnp.dot(lhs, rhs, preferred_element_type=F32)
        at = 0
        for f in frames:
            for r, n in spans:
                piece = d[at : at + n * wide].reshape(n, wide, 3 * ch)
                if first:
                    Y[f, r : r + n] = piece
                else:
                    Y[f, r : r + n] += piece
                at += n * wide

    def own(s, spans):
        taps(s, 2, (0, 1), spans, True)
        taps(s, 1, (1,), spans, False)

    def earlier(s, spans):
        taps(s, 1, (0,), spans, False)
        taps(s, 0, (0, 1), spans, False)

    def total(f, r):
        y = Y[f, r]
        return shift_down(y[:, :ch]) + y[:, ch : 2 * ch] + shift_up(y[:, 2 * ch :])

    def finish(s, spread):
        def step(i, c):
            f, j = i // 4, i % 4
            r = j + (j // 2) * 4 if spread else j + 2
            v = total(f, r)
            if s == 0:
                v = rms_silu(v)
            else:
                v = lat[f, r].astype(F32) + v
            X[s + 1, 2 + f, 1 + r] = v.astype(BF)
            return c

        lax.fori_loop(0, 8, step, 0, unroll=4)

    send_outer(0)
    send_inner(0)

    ws_copy.wait()
    co = ws.shape[2]
    for p in range(2):
        for k in range(3):
            wsp[p, :, 256 * k + co : 256 * (k + 1)] = jnp.zeros((2 * ch, 256 - co), BF)
    for p, half, bs in ((0, 0, (0,)), (0, 1, (1, 2)), (1, 0, (0, 1)), (1, 1, (2,))):
        es = []
        for e in range(3):
            v = ws[bs[0], e].astype(F32)
            for b in bs[1:]:
                v = v + ws[b, e].astype(F32)
            es.append(v)
        rows = pl.ds(half * ch, ch)
        for k, v in enumerate((es[0] + es[1] + es[2], es[0], es[2])):
            wsp[p, rows, 256 * k : 256 * k + co] = v.T.astype(BF)

    for s in range(2):
        wait_w(s, 2)
        wait_w(s, 1)
        own(s, INNER)
        wait_own_halo(s)
        forward(s)
        own(s, OUTER)
        wait_w(s, 0)
        wait_outer(s)
        earlier(s, OUTER)
        finish(s, True)
        send_outer(s + 1)
        wait_inner(s)
        earlier(s, INNER)
        finish(s, False)
        send_inner(s + 1)

    wt_copy.wait()
    wait_own_halo(2)
    forward(2)

    def double(spans):
        parts = []
        for a in range(3):
            rows = []
            for f in range(2):
                for r, n in spans:
                    rows.append(X[2, f + a, r : r + n].reshape(n * wide, ch))
            parts.append(jnp.concatenate(rows, axis=0))
        lhs = jnp.concatenate(parts, axis=1)
        rhs = jnp.concatenate([wt[a] for a in range(3)], axis=0)
        d = jnp.dot(lhs, rhs, preferred_element_type=F32).astype(BF)
        at = 0
        for f in range(2):
            for r, n in spans:
                for j in range(2):
                    U[2 * f + j, r : r + n] = d[at : at + n * wide, j * ch : (j + 1) * ch].reshape(n, wide, ch)
                at += n * wide

    def space(spans):
        rows_of = [r + k for r, n in spans for k in range(n)]

        def product(unit):
            p, f = unit
            parts = []
            for h in range(2):
                rows = [U[f, r + p + h : r + p + h + n].reshape(n * wide, ch) for r, n in spans]
                parts.append(jnp.concatenate(rows, axis=0))
            lhs = jnp.concatenate(parts, axis=1)
            d = jnp.dot(lhs, wsp[p], preferred_element_type=F32)
            Z[f] = d.reshape(4, wide, 768)

        def spread_columns(unit):
            p, f = unit
            for j, r in enumerate(rows_of):
                z = Z[f, j]
                mid, left, right = z[:, :256], z[:, 256:512], z[:, 512:]
                even = mid - left + shift_down(left)
                odd = mid - right + shift_up(right)
                for h in range(2):
                    T[j, h, pl.ds(0, wide, stride=2), :] = even[:, h * 128 : (h + 1) * 128]
                    T[j, h, pl.ds(1, wide, stride=2), :] = odd[:, h * 128 : (h + 1) * 128]
                out[f, 2 * r + p, :, 0:128] = T[j, 0].astype(BF)
                out[f, 2 * r + p, :, 128:co] = T[j, 1, :, 0 : co - 128].astype(BF)

        units = [(p, f) for p in range(2) for f in range(4)]
        product(units[0])
        for k in range(1, len(units)):
            product(units[k])
            spread_columns(units[k - 1])
        spread_columns(units[-1])

    wait_outer(2)
    double(((0, 4), (6, 4)))
    space(OUTER)
    wait_inner(2)
    double(((4, 2),))
    space(INNER)

    for s in range(3):
        @pl.when(has_next)
        def _():
            for k in range(NY):
                y_copy(s, k).wait_send()

        @pl.when(has_up)
        def _():
            t_copy(s, 0).wait_send()

            @pl.when(has_prev)
            def _():
                t_copy(s, 2).wait_send()

        @pl.when(has_down)
        def _():
            t_copy(s, 1).wait_send()

            @pl.when(has_prev)
            def _():
                t_copy(s, 3).wait_send()


def solution(mesh):
    tiles, groups = mesh.shape["tile"], mesh.shape["group"]

    def local(latent, conv_first, conv_second, time_weight, space_weight):
        frames, rows, wide, ch = latent.shape
        co = space_weight.shape[3]
        hbm = pl.BlockSpec(memory_space=pltpu.HBM)
        dma = pltpu.SemaphoreType.DMA
        return pl.pallas_call(
            functools.partial(kernel, tiles, groups),
            name="block",
            out_shape=pltpu.VMEM((2 * frames, 2 * rows, 2 * wide, co), BF),
            in_specs=[hbm] * 5,
            out_specs=pl.BlockSpec(memory_space=pltpu.VMEM),
            scratch_shapes=[
                pltpu.VMEM((2, 8, wide, ch), BF),
                pltpu.VMEM((3, 4, 10, wide, ch), BF),
                pltpu.VMEM((2, 3, 3, 3, ch, ch), BF),
                pltpu.VMEM((3, ch, 2 * ch), BF),
                pltpu.VMEM((3, 3, co, ch), BF),
                pltpu.VMEM((2, 2 * ch, 768), BF),
                pltpu.VMEM((2, 8, wide, 3 * ch), F32),
                pltpu.VMEM((4, 10, wide, ch), BF),
                pltpu.VMEM((4, 4, wide, 768), F32),
                pltpu.VMEM((4, 2, 2 * wide, 128), F32),
                dma,
                dma((2, 3, 3)),
                dma,
                dma,
                dma((3, NY)),
                dma((3, NY)),
                dma((3, 4)),
                dma((3, 4)),
            ],
            compiler_params=pltpu.CompilerParams(
                collective_id=0, has_side_effects=True, vmem_limit_bytes=51 * 2**20
            ),
        )(latent, conv_first, conv_second, time_weight, jnp.swapaxes(space_weight, 2, 3))

    return jax.shard_map(
        local,
        mesh=mesh,
        in_specs=(P("group", "tile", None, None), P(), P(), P(), P()),
        out_specs=P("group", "tile", None, None),
        check_vma=False,
    )
```

```python
import functools

import jax
import jax.numpy as jnp
from jax import lax
from jax.experimental import pallas as pl
from jax.experimental.pallas import tpu as pltpu
from jax.sharding import PartitionSpec as P

MESH = pl.DeviceIdType.MESH
BF = jnp.bfloat16
F32 = jnp.float32

OUTER = ((0, 2), (6, 2))
EDGES = ((0, 1), (7, 1))
MIDDLE = ((1, 1), (6, 1))
INNER = ((2, 4),)
SENDS = ((1, 1), (8, 1), (2, 1), (7, 1), (3, 1), (6, 1), (4, 2))
NY = len(SENDS)


def rms_silu(v):
    v = v * lax.rsqrt(jnp.mean(v * v, axis=-1, keepdims=True) + 1e-06)
    return v / (1.0 + jnp.exp(-v))


def shift_down(v):
    at = lax.broadcasted_iota(jnp.int32, v.shape, 0)
    return jnp.where(at == 0, 0.0, pltpu.roll(v, 1, 0))


def shift_up(v):
    at = lax.broadcasted_iota(jnp.int32, v.shape, 0)
    return jnp.where(at == v.shape[0] - 1, 0.0, pltpu.roll(v, v.shape[0] - 1, 0))


def kernel(
    tiles, groups,
    latent, conv_first, conv_second, time_weight, space_weight, out,
    lat, X, W, wt, ws, wsp, Y, U, Z, T,
    lat_sem, w_sem, wt_sem, ws_sem, y_send, y_recv, t_send, t_recv,
):
    t = lax.axis_index("tile")
    g = lax.axis_index("group")
    wide = lat.shape[2]
    ch = lat.shape[3]
    co = ws.shape[2]
    has_up, has_down = t > 0, t < tiles - 1
    has_prev, has_next = g > 0, g < groups - 1
    up = (lax.rem(t + tiles - 1, tiles), g)
    down = (lax.rem(t + 1, tiles), g)
    prev = (t, lax.rem(g + groups - 1, groups))
    after = (t, lax.rem(g + 1, groups))

    barrier = pltpu.get_barrier_semaphore()
    for other in (up, down, prev, after):
        pl.semaphore_signal(barrier, inc=1, device_id=other, device_id_type=MESH)

    lat_copy = pltpu.make_async_copy(latent, lat, lat_sem)
    lat_copy.start()
    w_copies = []
    for s, src in ((0, conv_first), (1, conv_second)):
        for a in (2, 1, 0):
            for b in range(3):
                w_copies.append(pltpu.make_async_copy(src.at[a, b], W.at[s, a, b], w_sem.at[s, a, b]))
    for c in w_copies[:6]:
        c.start()
    wt_copy = pltpu.make_async_copy(time_weight, wt, wt_sem)
    ws_copy = pltpu.make_async_copy(space_weight, ws, ws_sem)

    def wait_w(s, a):
        for b in range(3):
            pltpu.make_async_copy(conv_first.at[a, b], W.at[s, a, b], w_sem.at[s, a, b]).wait()

    @pl.when(jnp.logical_not(has_prev))
    def _():
        for s in range(3):
            for f in range(2):
                X[s, f] = jnp.zeros(X.shape[2:], BF)

    @pl.when(jnp.logical_not(has_up))
    def _():
        for s in range(3):
            X[s, :, 0] = jnp.zeros((4,) + X.shape[3:], BF)

    @pl.when(jnp.logical_not(has_down))
    def _():
        for s in range(3):
            X[s, :, 9] = jnp.zeros((4,) + X.shape[3:], BF)

    lat_copy.wait()

    def act_own(i, c):
        f, r = i // 8, i % 8
        X[0, 2 + f, 1 + r] = rms_silu(lat[f, r].astype(F32)).astype(BF)
        return c

    lax.fori_loop(0, 16, act_own, 0, unroll=4)

    pl.semaphore_wait(barrier, 4)

    def y_copy(s, k):
        row, count = SENDS[k]
        return pltpu.make_async_remote_copy(
            src_ref=X.at[s, pl.ds(2, 2), pl.ds(row, count)],
            dst_ref=X.at[s, pl.ds(0, 2), pl.ds(row, count)],
            send_sem=y_send.at[s, k],
            recv_sem=y_recv.at[s, k],
            device_id=after,
            device_id_type=MESH,
        )

    def t_copy(s, k):
        frame = 2 if k < 2 else 0
        row, slot, other = (1, 9, up) if k % 2 == 0 else (8, 0, down)
        return pltpu.make_async_remote_copy(
            src_ref=X.at[s, pl.ds(frame, 2), row],
            dst_ref=X.at[s, pl.ds(frame, 2), slot],
            send_sem=t_send.at[s, k],
            recv_sem=t_recv.at[s, k],
            device_id=other,
            device_id_type=MESH,
        )

    def send_edges(s):
        @pl.when(has_next)
        def _():
            y_copy(s, 0).start()
            y_copy(s, 1).start()

        @pl.when(has_up)
        def _():
            t_copy(s, 0).start()

        @pl.when(has_down)
        def _():
            t_copy(s, 1).start()

    def send_middle(s):
        @pl.when(has_next)
        def _():
            y_copy(s, 2).start()
            y_copy(s, 3).start()

    def send_inner(s):
        @pl.when(has_next)
        def _():
            for k in range(4, NY):
                y_copy(s, k).start()

    def wait_own_halo(s):
        @pl.when(has_down)
        def _():
            t_copy(s, 0).wait_recv()

        @pl.when(has_up)
        def _():
            t_copy(s, 1).wait_recv()

    def forward(s):
        @pl.when(has_prev)
        def _():
            y_copy(s, 0).wait_recv()

            @pl.when(has_up)
            def _():
                t_copy(s, 2).start()

            y_copy(s, 1).wait_recv()

            @pl.when(has_down)
            def _():
                t_copy(s, 3).start()

    def wait_edges(s):
        @pl.when(has_prev)
        def _():
            y_copy(s, 2).wait_recv()
            y_copy(s, 3).wait_recv()

            @pl.when(has_down)
            def _():
                t_copy(s, 2).wait_recv()

            @pl.when(has_up)
            def _():
                t_copy(s, 3).wait_recv()

    def wait_middle(s):
        @pl.when(has_prev)
        def _():
            y_copy(s, 4).wait_recv()
            y_copy(s, 5).wait_recv()

    def wait_inner(s):
        @pl.when(has_prev)
        def _():
            y_copy(s, NY - 1).wait_recv()

    def taps(s, a, frames, spans, first):
        parts = []
        for b in range(3):
            rows = []
            for f in frames:
                for r, n in spans:
                    rows.append(X[s, f + a, r + b : r + b + n].reshape(n * wide, ch))
            parts.append(jnp.concatenate(rows, axis=0))
        lhs = jnp.concatenate(parts, axis=1)
        rhs = jnp.concatenate(
            [jnp.concatenate([W[s, a, b, e] for e in range(3)], axis=1) for b in range(3)], axis=0
        )
        d = jnp.dot(lhs, rhs, preferred_element_type=F32)
        at = 0
        for f in frames:
            for r, n in spans:
                piece = d[at : at + n * wide].reshape(n, wide, 3 * ch)
                if first:
                    Y[f, r : r + n] = piece
                else:
                    Y[f, r : r + n] += piece
                at += n * wide

    def sum_taps():
        ws_copy.wait()
        for p in range(2):
            for k in range(3):
                wsp[p, :, 256 * k + co : 256 * (k + 1)] = jnp.zeros((2 * ch, 256 - co), BF)
        for p, half, bs in ((0, 0, (0,)), (0, 1, (1, 2)), (1, 0, (0, 1)), (1, 1, (2,))):
            es = []
            for e in range(3):
                v = ws[bs[0], e].astype(F32)
                for b in bs[1:]:
                    v = v + ws[b, e].astype(F32)
                es.append(v)
            rows = pl.ds(half * ch, ch)
            for k, v in enumerate((es[0] + es[1] + es[2], es[0], es[2])):
                wsp[p, rows, 256 * k : 256 * k + co] = v.T.astype(BF)

    def joined(s, f, steps, spans, first):
        parts = []
        for a in steps:
            for b in range(3):
                rows = [X[s, f + a, r + b : r + b + n].reshape(n * wide, ch) for r, n in spans]
                parts.append(jnp.concatenate(rows, axis=0))
        lhs = jnp.concatenate(parts, axis=1)
        rhs = jnp.concatenate(
            [jnp.concatenate([W[s, a, b, e] for e in range(3)], axis=1) for a in steps for b in range(3)], axis=0
        )
        d = jnp.dot(lhs, rhs, preferred_element_type=F32)
        at = 0
        for r, n in spans:
            piece = d[at : at + n * wide].reshape(n, wide, 3 * ch)
            if first:
                Y[f, r : r + n] = piece
            else:
                Y[f, r : r + n] += piece
            at += n * wide

    def own(s, spans):
        joined(s, 1, (1, 2), spans, True)
        joined(s, 0, (2,), spans, True)

    def earlier_small(s, spans):
        taps(s, 1, (0,), spans, False)
        taps(s, 0, (0, 1), spans, False)

    def earlier(s, spans):
        joined(s, 0, (0, 1), spans, False)
        joined(s, 1, (0,), spans, False)

    def total(f, r):
        y = Y[f, r]
        return shift_down(y[:, :ch]) + y[:, ch : 2 * ch] + shift_up(y[:, 2 * ch :])

    def finish(s, start, step, count):
        def one(i, c):
            f, r = i // count, start + step * (i % count)
            v = total(f, r)
            if s == 0:
                v = rms_silu(v)
            else:
                v = lat[f, r].astype(F32) + v
            X[s + 1, 2 + f, 1 + r] = v.astype(BF)
            return c

        lax.fori_loop(0, 2 * count, one, 0, unroll=4)

    send_edges(0)
    send_middle(0)
    send_inner(0)
    for c in w_copies[6:] + [ws_copy, wt_copy]:
        c.start()

    for s in range(2):
        wait_w(s, 2)
        wait_w(s, 1)
        own(s, INNER)
        wait_own_halo(s)
        forward(s)
        own(s, OUTER)
        wait_w(s, 0)
        wait_edges(s)
        earlier_small(s, EDGES)
        finish(s, 0, 7, 2)
        send_edges(s + 1)
        wait_middle(s)
        earlier_small(s, MIDDLE)
        finish(s, 1, 5, 2)
        send_middle(s + 1)
        wait_inner(s)
        earlier(s, INNER)
        finish(s, 2, 1, 4)
        send_inner(s + 1)

    sum_taps()
    wt_copy.wait()
    wait_own_halo(2)
    forward(2)

    def double(spans):
        parts = []
        for a in range(3):
            rows = []
            for f in range(2):
                for r, n in spans:
                    rows.append(X[2, f + a, r : r + n].reshape(n * wide, ch))
            parts.append(jnp.concatenate(rows, axis=0))
        lhs = jnp.concatenate(parts, axis=1)
        rhs = jnp.concatenate([wt[a] for a in range(3)], axis=0)
        d = jnp.dot(lhs, rhs, preferred_element_type=F32).astype(BF)
        at = 0
        for f in range(2):
            for r, n in spans:
                for j in range(2):
                    U[2 * f + j, r : r + n] = d[at : at + n * wide, j * ch : (j + 1) * ch].reshape(n, wide, ch)
                at += n * wide

    def space(spans):
        rows_of = [r + k for r, n in spans for k in range(n)]

        def product(unit):
            p, f = unit
            parts = []
            for h in range(2):
                rows = [U[f, r + p + h : r + p + h + n].reshape(n * wide, ch) for r, n in spans]
                parts.append(jnp.concatenate(rows, axis=0))
            lhs = jnp.concatenate(parts, axis=1)
            d = jnp.dot(lhs, wsp[p], preferred_element_type=F32)
            Z[f] = d.reshape(4, wide, 768)

        def spread_columns(unit):
            p, f = unit
            for j, r in enumerate(rows_of):
                z = Z[f, j]
                mid, left, right = z[:, :256], z[:, 256:512], z[:, 512:]
                even = mid - left + shift_down(left)
                odd = mid - right + shift_up(right)
                for h in range(2):
                    T[j, h, pl.ds(0, wide, stride=2), :] = even[:, h * 128 : (h + 1) * 128]
                    T[j, h, pl.ds(1, wide, stride=2), :] = odd[:, h * 128 : (h + 1) * 128]
                out[f, 2 * r + p, :, 0:128] = T[j, 0].astype(BF)
                out[f, 2 * r + p, :, 128:co] = T[j, 1, :, 0 : co - 128].astype(BF)

        units = [(p, f) for p in range(2) for f in range(4)]
        product(units[0])
        for k in range(1, len(units)):
            product(units[k])
            spread_columns(units[k - 1])
        spread_columns(units[-1])

    wait_edges(2)
    wait_middle(2)
    double(((0, 4), (6, 4)))
    space(OUTER)
    wait_inner(2)
    double(((4, 2),))
    space(INNER)

    for s in range(3):
        @pl.when(has_next)
        def _():
            for k in range(NY):
                y_copy(s, k).wait_send()

        @pl.when(has_up)
        def _():
            t_copy(s, 0).wait_send()

            @pl.when(has_prev)
            def _():
                t_copy(s, 2).wait_send()

        @pl.when(has_down)
        def _():
            t_copy(s, 1).wait_send()

            @pl.when(has_prev)
            def _():
                t_copy(s, 3).wait_send()


def solution(mesh):
    tiles, groups = mesh.shape["tile"], mesh.shape["group"]

    def local(latent, conv_first, conv_second, time_weight, space_weight):
        frames, rows, wide, ch = latent.shape
        co = space_weight.shape[3]
        hbm = pl.BlockSpec(memory_space=pltpu.HBM)
        dma = pltpu.SemaphoreType.DMA
        return pl.pallas_call(
            functools.partial(kernel, tiles, groups),
            name="block",
            out_shape=pltpu.VMEM((2 * frames, 2 * rows, 2 * wide, co), BF),
            in_specs=[hbm] * 5,
            out_specs=pl.BlockSpec(memory_space=pltpu.VMEM),
            scratch_shapes=[
                pltpu.VMEM((2, 8, wide, ch), BF),
                pltpu.VMEM((3, 4, 10, wide, ch), BF),
                pltpu.VMEM((2, 3, 3, 3, ch, ch), BF),
                pltpu.VMEM((3, ch, 2 * ch), BF),
                pltpu.VMEM((3, 3, co, ch), BF),
                pltpu.VMEM((2, 2 * ch, 768), BF),
                pltpu.VMEM((2, 8, wide, 3 * ch), F32),
                pltpu.VMEM((4, 10, wide, ch), BF),
                pltpu.VMEM((4, 4, wide, 768), F32),
                pltpu.VMEM((4, 2, 2 * wide, 128), F32),
                dma,
                dma((2, 3, 3)),
                dma,
                dma,
                dma((3, NY)),
                dma((3, NY)),
                dma((3, 4)),
                dma((3, 4)),
            ],
            compiler_params=pltpu.CompilerParams(
                collective_id=0, has_side_effects=True, vmem_limit_bytes=51 * 2**20
            ),
        )(latent, conv_first, conv_second, time_weight, jnp.swapaxes(space_weight, 2, 3))

    return jax.shard_map(
        local,
        mesh=mesh,
        in_specs=(P("group", "tile", None, None), P(), P(), P(), P()),
        out_specs=P("group", "tile", None, None),
        check_vma=False,
    )
```

```python
import functools

import jax
import jax.numpy as jnp
from jax import lax
from jax.experimental import pallas as pl
from jax.experimental.pallas import tpu as pltpu
from jax.sharding import PartitionSpec as P

MESH = pl.DeviceIdType.MESH
BF = jnp.bfloat16
F32 = jnp.float32

OUTER = ((0, 2), (6, 2))
EDGES = ((0, 1), (7, 1))
MIDDLE = ((1, 1), (6, 1))
INNER = ((2, 4),)
SENDS = ((1, 1), (8, 1), (2, 1), (7, 1), (3, 1), (6, 1), (4, 2))
NY = len(SENDS)


def rms_silu(v):
    v = v * lax.rsqrt(jnp.mean(v * v, axis=-1, keepdims=True) + 1e-06)
    return v / (1.0 + jnp.exp(-v))


def shift_down(v):
    at = lax.broadcasted_iota(jnp.int32, v.shape, 0)
    return jnp.where(at == 0, 0.0, pltpu.roll(v, 1, 0))


def shift_up(v):
    at = lax.broadcasted_iota(jnp.int32, v.shape, 0)
    return jnp.where(at == v.shape[0] - 1, 0.0, pltpu.roll(v, v.shape[0] - 1, 0))


def kernel(
    tiles, groups,
    latent, conv_first, conv_second, time_weight, space_weight, out,
    lat, X, W, wt, ws, wsp, Y, D, U, Z, T,
    lat_sem, w_sem, wt_sem, ws_sem, y_send, y_recv, t_send, t_recv,
):
    t = lax.axis_index("tile")
    g = lax.axis_index("group")
    wide = lat.shape[2]
    ch = lat.shape[3]
    co = ws.shape[2]
    has_up, has_down = t > 0, t < tiles - 1
    has_prev, has_next = g > 0, g < groups - 1
    up = (lax.rem(t + tiles - 1, tiles), g)
    down = (lax.rem(t + 1, tiles), g)
    prev = (t, lax.rem(g + groups - 1, groups))
    after = (t, lax.rem(g + 1, groups))

    barrier = pltpu.get_barrier_semaphore()
    for other in (up, down, prev, after):
        pl.semaphore_signal(barrier, inc=1, device_id=other, device_id_type=MESH)

    lat_copy = pltpu.make_async_copy(latent, lat, lat_sem)
    lat_copy.start()
    w_copies = []
    for s, src in ((0, conv_first), (1, conv_second)):
        for a in (2, 1, 0):
            for b in range(3):
                w_copies.append(pltpu.make_async_copy(src.at[a, b], W.at[s, a, b], w_sem.at[s, a, b]))
    for c in w_copies[:6]:
        c.start()
    wt_copy = pltpu.make_async_copy(time_weight, wt, wt_sem)
    ws_copy = pltpu.make_async_copy(space_weight, ws, ws_sem)

    def wait_w(s, a):
        for b in range(3):
            pltpu.make_async_copy(conv_first.at[a, b], W.at[s, a, b], w_sem.at[s, a, b]).wait()

    @pl.when(jnp.logical_not(has_prev))
    def _():
        for s in range(3):
            for f in range(2):
                X[s, f] = jnp.zeros(X.shape[2:], BF)

    @pl.when(jnp.logical_not(has_up))
    def _():
        for s in range(3):
            X[s, :, 0] = jnp.zeros((4,) + X.shape[3:], BF)

    @pl.when(jnp.logical_not(has_down))
    def _():
        for s in range(3):
            X[s, :, 9] = jnp.zeros((4,) + X.shape[3:], BF)

    lat_copy.wait()

    def act_own(i, c):
        f, r = i // 8, i % 8
        X[0, 2 + f, 1 + r] = rms_silu(lat[f, r].astype(F32)).astype(BF)
        return c

    lax.fori_loop(0, 16, act_own, 0, unroll=4)

    pl.semaphore_wait(barrier, 4)

    def y_copy(s, k):
        row, count = SENDS[k]
        return pltpu.make_async_remote_copy(
            src_ref=X.at[s, pl.ds(2, 2), pl.ds(row, count)],
            dst_ref=X.at[s, pl.ds(0, 2), pl.ds(row, count)],
            send_sem=y_send.at[s, k],
            recv_sem=y_recv.at[s, k],
            device_id=after,
            device_id_type=MESH,
        )

    def t_copy(s, k):
        frame = 2 if k < 2 else 0
        row, slot, other = (1, 9, up) if k % 2 == 0 else (8, 0, down)
        return pltpu.make_async_remote_copy(
            src_ref=X.at[s, pl.ds(frame, 2), row],
            dst_ref=X.at[s, pl.ds(frame, 2), slot],
            send_sem=t_send.at[s, k],
            recv_sem=t_recv.at[s, k],
            device_id=other,
            device_id_type=MESH,
        )

    def send_edges(s):
        @pl.when(has_up)
        def _():
            t_copy(s, 0).start()

        @pl.when(has_down)
        def _():
            t_copy(s, 1).start()

        @pl.when(has_next)
        def _():
            y_copy(s, 0).start()
            y_copy(s, 1).start()

    def send_middle(s):
        @pl.when(has_next)
        def _():
            y_copy(s, 2).start()
            y_copy(s, 3).start()

    def send_inner(s):
        @pl.when(has_next)
        def _():
            for k in range(4, NY):
                y_copy(s, k).start()

    def wait_own_halo(s):
        @pl.when(has_down)
        def _():
            t_copy(s, 0).wait_recv()

        @pl.when(has_up)
        def _():
            t_copy(s, 1).wait_recv()

    def forward(s):
        @pl.when(has_prev)
        def _():
            y_copy(s, 0).wait_recv()

            @pl.when(has_up)
            def _():
                t_copy(s, 2).start()

            y_copy(s, 1).wait_recv()

            @pl.when(has_down)
            def _():
                t_copy(s, 3).start()

    def wait_edges(s):
        @pl.when(has_prev)
        def _():
            y_copy(s, 2).wait_recv()
            y_copy(s, 3).wait_recv()

            @pl.when(has_down)
            def _():
                t_copy(s, 2).wait_recv()

            @pl.when(has_up)
            def _():
                t_copy(s, 3).wait_recv()

    def wait_middle(s):
        @pl.when(has_prev)
        def _():
            y_copy(s, 4).wait_recv()
            y_copy(s, 5).wait_recv()

    def wait_inner(s):
        @pl.when(has_prev)
        def _():
            y_copy(s, NY - 1).wait_recv()

    def taps(s, a, frames, spans, first):
        parts = []
        for b in range(3):
            rows = []
            for f in frames:
                for r, n in spans:
                    rows.append(X[s, f + a, r + b : r + b + n].reshape(n * wide, ch))
            parts.append(jnp.concatenate(rows, axis=0))
        lhs = jnp.concatenate(parts, axis=1)
        rhs = jnp.concatenate(
            [jnp.concatenate([W[s, a, b, e] for e in range(3)], axis=1) for b in range(3)], axis=0
        )
        d = jnp.dot(lhs, rhs, preferred_element_type=F32)
        at = 0
        for f in frames:
            for r, n in spans:
                piece = d[at : at + n * wide].reshape(n, wide, 3 * ch)
                if first:
                    Y[f, r : r + n] = piece
                else:
                    Y[f, r : r + n] += piece
                at += n * wide

    def sum_taps():
        ws_copy.wait()
        for p in range(2):
            for k in range(3):
                wsp[p, :, 256 * k + co : 256 * (k + 1)] = jnp.zeros((2 * ch, 256 - co), BF)
        for p, half, bs in ((0, 0, (0,)), (0, 1, (1, 2)), (1, 0, (0, 1)), (1, 1, (2,))):
            es = []
            for e in range(3):
                v = ws[bs[0], e].astype(F32)
                for b in bs[1:]:
                    v = v + ws[b, e].astype(F32)
                es.append(v)
            rows = pl.ds(half * ch, ch)
            for k, v in enumerate((es[0] + es[1] + es[2], es[0], es[2])):
                wsp[p, rows, 256 * k : 256 * k + co] = v.T.astype(BF)

    def joined(s, f, steps, spans, first):
        parts = []
        for a in steps:
            for b in range(3):
                rows = [X[s, f + a, r + b : r + b + n].reshape(n * wide, ch) for r, n in spans]
                parts.append(jnp.concatenate(rows, axis=0))
        lhs = jnp.concatenate(parts, axis=1)
        rhs = jnp.concatenate(
            [jnp.concatenate([W[s, a, b, e] for e in range(3)], axis=1) for a in steps for b in range(3)], axis=0
        )
        d = jnp.dot(lhs, rhs, preferred_element_type=F32)
        at = 0
        for r, n in spans:
            piece = d[at : at + n * wide].reshape(n, wide, 3 * ch)
            if first:
                Y[f, r : r + n] = piece
            else:
                Y[f, r : r + n] += piece
            at += n * wide

    def own(s, spans):
        joined(s, 1, (1, 2), spans, True)
        joined(s, 0, (2,), spans, True)

    def earlier_small(s, spans):
        taps(s, 1, (0,), spans, False)
        taps(s, 0, (0, 1), spans, False)

    def earlier(s, spans):
        joined(s, 0, (0, 1), spans, False)
        joined(s, 1, (0,), spans, False)

    def total(f, r):
        y = Y[f, r]
        return shift_down(y[:, :ch]) + y[:, ch : 2 * ch] + shift_up(y[:, 2 * ch :])

    def finish(s, start, step, count):
        def one(i, c):
            f, r = i // count, start + step * (i % count)
            v = total(f, r)
            if s == 0:
                v = rms_silu(v)
            else:
                v = lat[f, r].astype(F32) + v
            X[s + 1, 2 + f, 1 + r] = v.astype(BF)
            return c

        lax.fori_loop(0, 2 * count, one, 0, unroll=4)

    send_edges(0)
    send_middle(0)
    send_inner(0)
    for c in w_copies[6:] + [ws_copy, wt_copy]:
        c.start()

    for s in range(2):
        wait_w(s, 2)
        wait_w(s, 1)
        if s == 0:
            own(s, INNER)
            forward(s)
        else:
            forward(s)
            own(s, INNER)
        wait_own_halo(s)
        own(s, OUTER)
        wait_w(s, 0)
        wait_edges(s)
        earlier_small(s, EDGES)
        finish(s, 0, 7, 2)
        send_edges(s + 1)
        wait_middle(s)
        earlier_small(s, MIDDLE)
        finish(s, 1, 5, 2)
        send_middle(s + 1)
        wait_inner(s)
        earlier(s, INNER)
        finish(s, 2, 1, 4)
        send_inner(s + 1)

    forward(2)
    sum_taps()
    wt_copy.wait()
    wait_own_halo(2)

    def time_product(f, steps, spans):
        parts = []
        for a in steps:
            rows = [X[2, f + a, r : r + n].reshape(n * wide, ch) for r, n in spans]
            parts.append(jnp.concatenate(rows, axis=0))
        lhs = jnp.concatenate(parts, axis=1)
        rhs = jnp.concatenate([wt[a] for a in steps], axis=0)
        return jnp.dot(lhs, rhs, preferred_element_type=F32)

    def double(spans):
        for f, steps in ((0, (0, 1)), (1, (0,))):
            d = time_product(f, steps, spans)
            at = 0
            for r, n in spans:
                v = (d[at : at + n * wide].reshape(n, wide, 2 * ch) + D[f, r : r + n]).astype(BF)
                for j in range(2):
                    U[2 * f + j, r : r + n] = v[:, :, j * ch : (j + 1) * ch]
                at += n * wide

    def space(spans):
        rows_of = [r + k for r, n in spans for k in range(n)]

        def product(unit):
            p, f = unit
            parts = []
            for h in range(2):
                rows = [U[f, r + p + h : r + p + h + n].reshape(n * wide, ch) for r, n in spans]
                parts.append(jnp.concatenate(rows, axis=0))
            lhs = jnp.concatenate(parts, axis=1)
            d = jnp.dot(lhs, wsp[p], preferred_element_type=F32)
            Z[f] = d.reshape(4, wide, 768)

        def spread_columns(unit):
            p, f = unit
            for j, r in enumerate(rows_of):
                z = Z[f, j]
                mid, left, right = z[:, :256], z[:, 256:512], z[:, 512:]
                even = mid - left + shift_down(left)
                odd = mid - right + shift_up(right)
                for h in range(2):
                    T[j, h, pl.ds(0, wide, stride=2), :] = even[:, h * 128 : (h + 1) * 128]
                    T[j, h, pl.ds(1, wide, stride=2), :] = odd[:, h * 128 : (h + 1) * 128]
                out[f, 2 * r + p, :, 0:128] = T[j, 0].astype(BF)
                out[f, 2 * r + p, :, 128:co] = T[j, 1, :, 0 : co - 128].astype(BF)

        units = [(p, f) for p in range(2) for f in range(4)]
        product(units[0])
        for k in range(1, len(units)):
            product(units[k])
            spread_columns(units[k - 1])
        spread_columns(units[-1])

    D[0] = time_product(0, (2,), ((0, 10),)).reshape(10, wide, 2 * ch)
    D[1] = time_product(1, (1, 2), ((0, 10),)).reshape(10, wide, 2 * ch)
    wait_edges(2)
    wait_middle(2)
    double(((0, 4), (6, 4)))
    space(OUTER)
    wait_inner(2)
    double(((4, 2),))
    space(INNER)

    for s in range(3):
        @pl.when(has_next)
        def _():
            for k in range(NY):
                y_copy(s, k).wait_send()

        @pl.when(has_up)
        def _():
            t_copy(s, 0).wait_send()

            @pl.when(has_prev)
            def _():
                t_copy(s, 2).wait_send()

        @pl.when(has_down)
        def _():
            t_copy(s, 1).wait_send()

            @pl.when(has_prev)
            def _():
                t_copy(s, 3).wait_send()


def solution(mesh):
    tiles, groups = mesh.shape["tile"], mesh.shape["group"]

    def local(latent, conv_first, conv_second, time_weight, space_weight):
        frames, rows, wide, ch = latent.shape
        co = space_weight.shape[3]
        hbm = pl.BlockSpec(memory_space=pltpu.HBM)
        dma = pltpu.SemaphoreType.DMA
        return pl.pallas_call(
            functools.partial(kernel, tiles, groups),
            name="block",
            out_shape=pltpu.VMEM((2 * frames, 2 * rows, 2 * wide, co), BF),
            in_specs=[hbm] * 5,
            out_specs=pl.BlockSpec(memory_space=pltpu.VMEM),
            scratch_shapes=[
                pltpu.VMEM((2, 8, wide, ch), BF),
                pltpu.VMEM((3, 4, 10, wide, ch), BF),
                pltpu.VMEM((2, 3, 3, 3, ch, ch), BF),
                pltpu.VMEM((3, ch, 2 * ch), BF),
                pltpu.VMEM((3, 3, co, ch), BF),
                pltpu.VMEM((2, 2 * ch, 768), BF),
                pltpu.VMEM((2, 8, wide, 3 * ch), F32),
                pltpu.VMEM((2, 10, wide, 2 * ch), F32),
                pltpu.VMEM((4, 10, wide, ch), BF),
                pltpu.VMEM((4, 4, wide, 768), F32),
                pltpu.VMEM((4, 2, 2 * wide, 128), F32),
                dma,
                dma((2, 3, 3)),
                dma,
                dma,
                dma((3, NY)),
                dma((3, NY)),
                dma((3, 4)),
                dma((3, 4)),
            ],
            compiler_params=pltpu.CompilerParams(
                collective_id=0, has_side_effects=True, vmem_limit_bytes=51 * 2**20
            ),
        )(latent, conv_first, conv_second, time_weight, jnp.swapaxes(space_weight, 2, 3))

    return jax.shard_map(
        local,
        mesh=mesh,
        in_specs=(P("group", "tile", None, None), P(), P(), P(), P()),
        out_specs=P("group", "tile", None, None),
        check_vma=False,
    )
```

```python
import functools

import jax
import jax.numpy as jnp
from jax import lax
from jax.experimental import pallas as pl
from jax.experimental.pallas import tpu as pltpu
from jax.sharding import PartitionSpec as P

MESH = pl.DeviceIdType.MESH
BF = jnp.bfloat16
F32 = jnp.float32

OUTER = ((0, 2), (6, 2))
EDGES = ((0, 1), (7, 1))
MIDDLE = ((1, 1), (6, 1))
INNER = ((2, 4),)
SENDS = ((1, 1), (8, 1), (2, 1), (7, 1), (3, 1), (6, 1), (4, 2))
NY = len(SENDS)


def rms_silu(v):
    v = v * lax.rsqrt(jnp.mean(v * v, axis=-1, keepdims=True) + 1e-06)
    return v / (1.0 + jnp.exp(-v))


def shift_down(v):
    at = lax.broadcasted_iota(jnp.int32, v.shape, 0)
    return jnp.where(at == 0, 0.0, pltpu.roll(v, 1, 0))


def shift_up(v):
    at = lax.broadcasted_iota(jnp.int32, v.shape, 0)
    return jnp.where(at == v.shape[0] - 1, 0.0, pltpu.roll(v, v.shape[0] - 1, 0))


def kernel(
    tiles, groups,
    latent, conv_first, conv_second, time_weight, space_weight, out,
    lat, X, W, wt, ws, wsp, Y, D, U, Z, T,
    lat_sem, w_sem, wt_sem, ws_sem, y_send, y_recv, t_send, t_recv,
):
    t = lax.axis_index("tile")
    g = lax.axis_index("group")
    wide = lat.shape[2]
    ch = lat.shape[3]
    co = ws.shape[2]
    has_up, has_down = t > 0, t < tiles - 1
    has_prev, has_next = g > 0, g < groups - 1
    up = (lax.rem(t + tiles - 1, tiles), g)
    down = (lax.rem(t + 1, tiles), g)
    prev = (t, lax.rem(g + groups - 1, groups))
    after = (t, lax.rem(g + 1, groups))

    barrier = pltpu.get_barrier_semaphore()
    for other in (up, down, prev, after):
        pl.semaphore_signal(barrier, inc=1, device_id=other, device_id_type=MESH)

    lat_copy = pltpu.make_async_copy(latent, lat, lat_sem)
    lat_copy.start()
    w_copies = []
    for s, src in ((0, conv_first), (1, conv_second)):
        for a in (2, 1, 0):
            for b in range(3):
                w_copies.append(pltpu.make_async_copy(src.at[a, b], W.at[s, a, b], w_sem.at[s, a, b]))
    for c in w_copies[:6]:
        c.start()
    wt_copy = pltpu.make_async_copy(time_weight, wt, wt_sem)
    ws_copy = pltpu.make_async_copy(space_weight, ws, ws_sem)

    def wait_w(s, a):
        for b in range(3):
            pltpu.make_async_copy(conv_first.at[a, b], W.at[s, a, b], w_sem.at[s, a, b]).wait()

    @pl.when(jnp.logical_not(has_prev))
    def _():
        for s in range(3):
            for f in range(2):
                X[s, f] = jnp.zeros(X.shape[2:], BF)

    @pl.when(jnp.logical_not(has_up))
    def _():
        for s in range(3):
            X[s, :, 0] = jnp.zeros((4,) + X.shape[3:], BF)

    @pl.when(jnp.logical_not(has_down))
    def _():
        for s in range(3):
            X[s, :, 9] = jnp.zeros((4,) + X.shape[3:], BF)

    lat_copy.wait()

    def act_own(i, c):
        f, r = i // 8, i % 8
        X[0, 2 + f, 1 + r] = rms_silu(lat[f, r].astype(F32)).astype(BF)
        return c

    lax.fori_loop(0, 16, act_own, 0, unroll=4)

    pl.semaphore_wait(barrier, 4)

    def y_copy(s, k):
        row, count = SENDS[k]
        return pltpu.make_async_remote_copy(
            src_ref=X.at[s, pl.ds(2, 2), pl.ds(row, count)],
            dst_ref=X.at[s, pl.ds(0, 2), pl.ds(row, count)],
            send_sem=y_send.at[s, k],
            recv_sem=y_recv.at[s, k],
            device_id=after,
            device_id_type=MESH,
        )

    def t_copy(s, k):
        frame = 2 if k < 2 else 0
        row, slot, other = (1, 9, up) if k % 2 == 0 else (8, 0, down)
        return pltpu.make_async_remote_copy(
            src_ref=X.at[s, pl.ds(frame, 2), row],
            dst_ref=X.at[s, pl.ds(frame, 2), slot],
            send_sem=t_send.at[s, k],
            recv_sem=t_recv.at[s, k],
            device_id=other,
            device_id_type=MESH,
        )

    def send_edges(s):
        @pl.when(has_up)
        def _():
            t_copy(s, 0).start()

        @pl.when(has_down)
        def _():
            t_copy(s, 1).start()

        @pl.when(has_next)
        def _():
            y_copy(s, 0).start()
            y_copy(s, 1).start()

    def send_middle(s):
        @pl.when(has_next)
        def _():
            y_copy(s, 2).start()
            y_copy(s, 3).start()

    def send_inner(s):
        @pl.when(has_next)
        def _():
            for k in range(4, NY):
                y_copy(s, k).start()

    def wait_own_halo(s):
        @pl.when(has_down)
        def _():
            t_copy(s, 0).wait_recv()

        @pl.when(has_up)
        def _():
            t_copy(s, 1).wait_recv()

    def forward(s):
        @pl.when(has_prev)
        def _():
            y_copy(s, 0).wait_recv()

            @pl.when(has_up)
            def _():
                t_copy(s, 2).start()

            y_copy(s, 1).wait_recv()

            @pl.when(has_down)
            def _():
                t_copy(s, 3).start()

    def wait_edges(s):
        @pl.when(has_prev)
        def _():
            y_copy(s, 2).wait_recv()
            y_copy(s, 3).wait_recv()

            @pl.when(has_down)
            def _():
                t_copy(s, 2).wait_recv()

            @pl.when(has_up)
            def _():
                t_copy(s, 3).wait_recv()

    def wait_middle(s):
        @pl.when(has_prev)
        def _():
            y_copy(s, 4).wait_recv()
            y_copy(s, 5).wait_recv()

    def wait_inner(s):
        @pl.when(has_prev)
        def _():
            y_copy(s, NY - 1).wait_recv()

    def taps(s, a, frames, spans, first):
        parts = []
        for b in range(3):
            rows = []
            for f in frames:
                for r, n in spans:
                    rows.append(X[s, f + a, r + b : r + b + n].reshape(n * wide, ch))
            parts.append(jnp.concatenate(rows, axis=0))
        lhs = jnp.concatenate(parts, axis=1)
        rhs = jnp.concatenate(
            [jnp.concatenate([W[s, a, b, e] for e in range(3)], axis=1) for b in range(3)], axis=0
        )
        d = jnp.dot(lhs, rhs, preferred_element_type=F32)
        at = 0
        for f in frames:
            for r, n in spans:
                piece = d[at : at + n * wide].reshape(n, wide, 3 * ch)
                if first:
                    Y[f, r : r + n] = piece
                else:
                    Y[f, r : r + n] += piece
                at += n * wide

    def sum_taps():
        ws_copy.wait()
        for p in range(2):
            for k in range(3):
                wsp[p, :, 256 * k + co : 256 * (k + 1)] = jnp.zeros((2 * ch, 256 - co), BF)
        for p, half, bs in ((0, 0, (0,)), (0, 1, (1, 2)), (1, 0, (0, 1)), (1, 1, (2,))):
            es = []
            for e in range(3):
                v = ws[bs[0], e].astype(F32)
                for b in bs[1:]:
                    v = v + ws[b, e].astype(F32)
                es.append(v)
            rows = pl.ds(half * ch, ch)
            for k, v in enumerate((es[0] + es[1] + es[2], es[0], es[2])):
                wsp[p, rows, 256 * k : 256 * k + co] = v.T.astype(BF)

    def joined(s, f, steps, spans, first):
        parts = []
        for a in steps:
            for b in range(3):
                rows = [X[s, f + a, r + b : r + b + n].reshape(n * wide, ch) for r, n in spans]
                parts.append(jnp.concatenate(rows, axis=0))
        lhs = jnp.concatenate(parts, axis=1)
        rhs = jnp.concatenate(
            [jnp.concatenate([W[s, a, b, e] for e in range(3)], axis=1) for a in steps for b in range(3)], axis=0
        )
        d = jnp.dot(lhs, rhs, preferred_element_type=F32)
        at = 0
        for r, n in spans:
            piece = d[at : at + n * wide].reshape(n, wide, 3 * ch)
            if first:
                Y[f, r : r + n] = piece
            else:
                Y[f, r : r + n] += piece
            at += n * wide

    def own(s, spans):
        joined(s, 1, (1, 2), spans, True)
        joined(s, 0, (2,), spans, True)

    def earlier_small(s, spans):
        taps(s, 1, (0,), spans, False)
        taps(s, 0, (0, 1), spans, False)

    def earlier(s, spans):
        joined(s, 0, (0, 1), spans, False)
        joined(s, 1, (0,), spans, False)

    def total(f, r):
        y = Y[f, r]
        return shift_down(y[:, :ch]) + y[:, ch : 2 * ch] + shift_up(y[:, 2 * ch :])

    def finish(s, start, step, count):
        def one(i, c):
            f, r = i // count, start + step * (i % count)
            v = total(f, r)
            if s == 0:
                v = rms_silu(v)
            else:
                v = lat[f, r].astype(F32) + v
            X[s + 1, 2 + f, 1 + r] = v.astype(BF)
            return c

        lax.fori_loop(0, 2 * count, one, 0, unroll=4)

    send_edges(0)
    send_middle(0)
    send_inner(0)
    for c in w_copies[6:15]:
        c.start()

    for s in range(2):
        wait_w(s, 2)
        wait_w(s, 1)
        if s == 0:
            own(s, INNER)
            forward(s)
        else:
            forward(s)
            own(s, INNER)
        wait_own_halo(s)
        own(s, OUTER)
        wait_w(s, 0)
        wait_edges(s)
        earlier_small(s, EDGES)
        finish(s, 0, 7, 2)
        send_edges(s + 1)
        wait_middle(s)
        earlier_small(s, MIDDLE)
        finish(s, 1, 5, 2)
        send_middle(s + 1)
        if s == 0:
            for c in w_copies[15:]:
                c.start()
        wait_inner(s)
        earlier(s, INNER)
        finish(s, 2, 1, 4)
        send_inner(s + 1)
        if s == 0:
            ws_copy.start()
            wt_copy.start()

    forward(2)
    sum_taps()
    wt_copy.wait()
    wait_own_halo(2)

    def time_product(f, steps, spans):
        parts = []
        for a in steps:
            rows = [X[2, f + a, r : r + n].reshape(n * wide, ch) for r, n in spans]
            parts.append(jnp.concatenate(rows, axis=0))
        lhs = jnp.concatenate(parts, axis=1)
        rhs = jnp.concatenate([wt[a] for a in steps], axis=0)
        return jnp.dot(lhs, rhs, preferred_element_type=F32)

    def double(spans):
        for f, steps in ((0, (0, 1)), (1, (0,))):
            d = time_product(f, steps, spans)
            at = 0
            for r, n in spans:
                v = (d[at : at + n * wide].reshape(n, wide, 2 * ch) + D[f, r : r + n]).astype(BF)
                for j in range(2):
                    U[2 * f + j, r : r + n] = v[:, :, j * ch : (j + 1) * ch]
                at += n * wide

    def space(spans):
        rows_of = [r + k for r, n in spans for k in range(n)]

        def product(unit):
            p, f = unit
            parts = []
            for h in range(2):
                rows = [U[f, r + p + h : r + p + h + n].reshape(n * wide, ch) for r, n in spans]
                parts.append(jnp.concatenate(rows, axis=0))
            lhs = jnp.concatenate(parts, axis=1)
            d = jnp.dot(lhs, wsp[p], preferred_element_type=F32)
            Z[f] = d.reshape(4, wide, 768)

        def spread_columns(unit):
            p, f = unit
            for j, r in enumerate(rows_of):
                z = Z[f, j]
                mid, left, right = z[:, :256], z[:, 256:512], z[:, 512:]
                even = mid - left + shift_down(left)
                odd = mid - right + shift_up(right)
                for h in range(2):
                    T[j, h, pl.ds(0, wide, stride=2), :] = even[:, h * 128 : (h + 1) * 128]
                    T[j, h, pl.ds(1, wide, stride=2), :] = odd[:, h * 128 : (h + 1) * 128]
                out[f, 2 * r + p, :, 0:128] = T[j, 0].astype(BF)
                out[f, 2 * r + p, :, 128:co] = T[j, 1, :, 0 : co - 128].astype(BF)

        units = [(p, f) for p in range(2) for f in range(4)]
        product(units[0])
        for k in range(1, len(units)):
            product(units[k])
            spread_columns(units[k - 1])
        spread_columns(units[-1])

    D[0] = time_product(0, (2,), ((0, 10),)).reshape(10, wide, 2 * ch)
    D[1] = time_product(1, (1, 2), ((0, 10),)).reshape(10, wide, 2 * ch)
    wait_edges(2)
    wait_middle(2)
    double(((0, 4), (6, 4)))
    space(OUTER)
    wait_inner(2)
    double(((4, 2),))
    space(INNER)

    for s in range(3):
        @pl.when(has_next)
        def _():
            for k in range(NY):
                y_copy(s, k).wait_send()

        @pl.when(has_up)
        def _():
            t_copy(s, 0).wait_send()

            @pl.when(has_prev)
            def _():
                t_copy(s, 2).wait_send()

        @pl.when(has_down)
        def _():
            t_copy(s, 1).wait_send()

            @pl.when(has_prev)
            def _():
                t_copy(s, 3).wait_send()


def solution(mesh):
    tiles, groups = mesh.shape["tile"], mesh.shape["group"]

    def local(latent, conv_first, conv_second, time_weight, space_weight):
        frames, rows, wide, ch = latent.shape
        co = space_weight.shape[3]
        hbm = pl.BlockSpec(memory_space=pltpu.HBM)
        dma = pltpu.SemaphoreType.DMA
        return pl.pallas_call(
            functools.partial(kernel, tiles, groups),
            name="block",
            out_shape=pltpu.VMEM((2 * frames, 2 * rows, 2 * wide, co), BF),
            in_specs=[hbm] * 5,
            out_specs=pl.BlockSpec(memory_space=pltpu.VMEM),
            scratch_shapes=[
                pltpu.VMEM((2, 8, wide, ch), BF),
                pltpu.VMEM((3, 4, 10, wide, ch), BF),
                pltpu.VMEM((2, 3, 3, 3, ch, ch), BF),
                pltpu.VMEM((3, ch, 2 * ch), BF),
                pltpu.VMEM((3, 3, co, ch), BF),
                pltpu.VMEM((2, 2 * ch, 768), BF),
                pltpu.VMEM((2, 8, wide, 3 * ch), F32),
                pltpu.VMEM((2, 10, wide, 2 * ch), F32),
                pltpu.VMEM((4, 10, wide, ch), BF),
                pltpu.VMEM((4, 4, wide, 768), F32),
                pltpu.VMEM((4, 2, 2 * wide, 128), F32),
                dma,
                dma((2, 3, 3)),
                dma,
                dma,
                dma((3, NY)),
                dma((3, NY)),
                dma((3, 4)),
                dma((3, 4)),
            ],
            compiler_params=pltpu.CompilerParams(
                collective_id=0, has_side_effects=True, vmem_limit_bytes=51 * 2**20
            ),
        )(latent, conv_first, conv_second, time_weight, jnp.swapaxes(space_weight, 2, 3))

    return jax.shard_map(
        local,
        mesh=mesh,
        in_specs=(P("group", "tile", None, None), P(), P(), P(), P()),
        out_specs=P("group", "tile", None, None),
        check_vma=False,
    )
```

```python
import functools

import jax
import jax.numpy as jnp
from jax import lax
from jax.experimental import pallas as pl
from jax.experimental.pallas import tpu as pltpu
from jax.sharding import PartitionSpec as P

MESH = pl.DeviceIdType.MESH
BF = jnp.bfloat16
F32 = jnp.float32

OUTER = ((0, 2), (6, 2))
EDGES = ((0, 1), (7, 1))
MIDDLE = ((1, 1), (6, 1))
INNER = ((2, 4),)
SENDS = ((1, 1), (8, 1), (2, 1), (7, 1), (3, 1), (6, 1), (4, 2))
NY = len(SENDS)


def rms_silu(v):
    v = v * lax.rsqrt(jnp.mean(v * v, axis=-1, keepdims=True) + 1e-06)
    return v / (1.0 + jnp.exp(-v))


def shift_down(v):
    at = lax.broadcasted_iota(jnp.int32, v.shape, 0)
    return jnp.where(at == 0, 0.0, pltpu.roll(v, 1, 0))


def shift_up(v):
    at = lax.broadcasted_iota(jnp.int32, v.shape, 0)
    return jnp.where(at == v.shape[0] - 1, 0.0, pltpu.roll(v, v.shape[0] - 1, 0))


def kernel(
    tiles, groups,
    latent, conv_first, conv_second, time_weight, space_weight, out,
    lat, X, W, wt, ws, wsp, Y, D, U, Z, T,
    lat_sem, w_sem, wt_sem, ws_sem, y_send, y_recv, t_send, t_recv,
):
    t = lax.axis_index("tile")
    g = lax.axis_index("group")
    wide = lat.shape[2]
    ch = lat.shape[3]
    co = ws.shape[2]
    has_up, has_down = t > 0, t < tiles - 1
    has_prev, has_next = g > 0, g < groups - 1
    up = (lax.rem(t + tiles - 1, tiles), g)
    down = (lax.rem(t + 1, tiles), g)
    prev = (t, lax.rem(g + groups - 1, groups))
    after = (t, lax.rem(g + 1, groups))

    barrier = pltpu.get_barrier_semaphore()
    for other in (up, down, prev, after):
        pl.semaphore_signal(barrier, inc=1, device_id=other, device_id_type=MESH)

    lat_copy = pltpu.make_async_copy(latent, lat, lat_sem)
    lat_copy.start()
    w_copies = []
    for s, src in ((0, conv_first), (1, conv_second)):
        for a in (2, 1, 0):
            for b in range(3):
                w_copies.append(pltpu.make_async_copy(src.at[a, b], W.at[s, a, b], w_sem.at[s, a, b]))
    for c in w_copies[:6]:
        c.start()
    wt_copy = pltpu.make_async_copy(time_weight, wt, wt_sem)
    ws_copy = pltpu.make_async_copy(space_weight, ws, ws_sem)

    def wait_w(s, a):
        for b in range(3):
            pltpu.make_async_copy(conv_first.at[a, b], W.at[s, a, b], w_sem.at[s, a, b]).wait()

    @pl.when(jnp.logical_not(has_prev))
    def _():
        for s in range(3):
            for f in range(2):
                X[s, f] = jnp.zeros(X.shape[2:], BF)

    @pl.when(jnp.logical_not(has_up))
    def _():
        for s in range(3):
            X[s, :, 0] = jnp.zeros((4,) + X.shape[3:], BF)

    @pl.when(jnp.logical_not(has_down))
    def _():
        for s in range(3):
            X[s, :, 9] = jnp.zeros((4,) + X.shape[3:], BF)

    lat_copy.wait()

    def act_own(i, c):
        f, r = i // 8, i % 8
        X[0, 2 + f, 1 + r] = rms_silu(lat[f, r].astype(F32)).astype(BF)
        return c

    lax.fori_loop(0, 16, act_own, 0, unroll=4)

    pl.semaphore_wait(barrier, 4)

    def y_copy(s, k):
        row, count = SENDS[k]
        return pltpu.make_async_remote_copy(
            src_ref=X.at[s, pl.ds(2, 2), pl.ds(row, count)],
            dst_ref=X.at[s, pl.ds(0, 2), pl.ds(row, count)],
            send_sem=y_send.at[s, k],
            recv_sem=y_recv.at[s, k],
            device_id=after,
            device_id_type=MESH,
        )

    def t_copy(s, k):
        frame = 2 if k < 2 else 0
        row, slot, other = (1, 9, up) if k % 2 == 0 else (8, 0, down)
        return pltpu.make_async_remote_copy(
            src_ref=X.at[s, pl.ds(frame, 2), row],
            dst_ref=X.at[s, pl.ds(frame, 2), slot],
            send_sem=t_send.at[s, k],
            recv_sem=t_recv.at[s, k],
            device_id=other,
            device_id_type=MESH,
        )

    def send_edges(s):
        @pl.when(has_up)
        def _():
            t_copy(s, 0).start()

        @pl.when(has_down)
        def _():
            t_copy(s, 1).start()

        @pl.when(has_next)
        def _():
            y_copy(s, 0).start()
            y_copy(s, 1).start()

    def send_middle(s):
        @pl.when(has_next)
        def _():
            y_copy(s, 2).start()
            y_copy(s, 3).start()

    def send_inner(s):
        @pl.when(has_next)
        def _():
            for k in range(4, NY):
                y_copy(s, k).start()

    def wait_own_halo(s):
        @pl.when(has_down)
        def _():
            t_copy(s, 0).wait_recv()

        @pl.when(has_up)
        def _():
            t_copy(s, 1).wait_recv()

    def forward(s):
        @pl.when(has_prev)
        def _():
            y_copy(s, 0).wait_recv()

            @pl.when(has_up)
            def _():
                t_copy(s, 2).start()

            y_copy(s, 1).wait_recv()

            @pl.when(has_down)
            def _():
                t_copy(s, 3).start()

    def wait_edges(s):
        @pl.when(has_prev)
        def _():
            y_copy(s, 2).wait_recv()
            y_copy(s, 3).wait_recv()

            @pl.when(has_down)
            def _():
                t_copy(s, 2).wait_recv()

            @pl.when(has_up)
            def _():
                t_copy(s, 3).wait_recv()

    def wait_middle(s):
        @pl.when(has_prev)
        def _():
            y_copy(s, 4).wait_recv()
            y_copy(s, 5).wait_recv()

    def wait_inner(s):
        @pl.when(has_prev)
        def _():
            y_copy(s, NY - 1).wait_recv()

    def taps(s, a, frames, spans, first):
        parts = []
        for b in range(3):
            rows = []
            for f in frames:
                for r, n in spans:
                    rows.append(X[s, f + a, r + b : r + b + n].reshape(n * wide, ch))
            parts.append(jnp.concatenate(rows, axis=0))
        lhs = jnp.concatenate(parts, axis=1)
        rhs = jnp.concatenate(
            [jnp.concatenate([W[s, a, b, e] for e in range(3)], axis=1) for b in range(3)], axis=0
        )
        d = jnp.dot(lhs, rhs, preferred_element_type=F32)
        at = 0
        for f in frames:
            for r, n in spans:
                piece = d[at : at + n * wide].reshape(n, wide, 3 * ch)
                if first:
                    Y[f, r : r + n] = piece
                else:
                    Y[f, r : r + n] += piece
                at += n * wide

    def sum_taps():
        ws_copy.wait()
        for p in range(2):
            for k in range(3):
                wsp[p, :, 256 * k + co : 256 * (k + 1)] = jnp.zeros((2 * ch, 256 - co), BF)
        for p, half, bs in ((0, 0, (0,)), (0, 1, (1, 2)), (1, 0, (0, 1)), (1, 1, (2,))):
            es = []
            for e in range(3):
                v = ws[bs[0], e].astype(F32)
                for b in bs[1:]:
                    v = v + ws[b, e].astype(F32)
                es.append(v)
            rows = pl.ds(half * ch, ch)
            for k, v in enumerate((es[0] + es[1] + es[2], es[0], es[2])):
                wsp[p, rows, 256 * k : 256 * k + co] = v.T.astype(BF)

    def joined(s, f, steps, spans, first):
        parts = []
        for a in steps:
            for b in range(3):
                rows = [X[s, f + a, r + b : r + b + n].reshape(n * wide, ch) for r, n in spans]
                parts.append(jnp.concatenate(rows, axis=0))
        lhs = jnp.concatenate(parts, axis=1)
        rhs = jnp.concatenate(
            [jnp.concatenate([W[s, a, b, e] for e in range(3)], axis=1) for a in steps for b in range(3)], axis=0
        )
        d = jnp.dot(lhs, rhs, preferred_element_type=F32)
        at = 0
        for r, n in spans:
            piece = d[at : at + n * wide].reshape(n, wide, 3 * ch)
            if first:
                Y[f, r : r + n] = piece
            else:
                Y[f, r : r + n] += piece
            at += n * wide

    def own(s, spans):
        joined(s, 1, (1, 2), spans, True)
        joined(s, 0, (2,), spans, True)

    def earlier_small(s, spans):
        taps(s, 1, (0,), spans, False)
        taps(s, 0, (0, 1), spans, False)

    def earlier(s, spans):
        joined(s, 0, (0, 1), spans, False)
        joined(s, 1, (0,), spans, False)

    def total(f, r):
        y = Y[f, r]
        return shift_down(y[:, :ch]) + y[:, ch : 2 * ch] + shift_up(y[:, 2 * ch :])

    def finish(s, start, step, count):
        def one(i, c):
            f, r = i // count, start + step * (i % count)
            v = total(f, r)
            if s == 0:
                v = rms_silu(v)
            else:
                v = lat[f, r].astype(F32) + v
            X[s + 1, 2 + f, 1 + r] = v.astype(BF)
            return c

        lax.fori_loop(0, 2 * count, one, 0, unroll=4)

    send_edges(0)
    send_middle(0)
    send_inner(0)
    for c in w_copies[6:] + [ws_copy, wt_copy]:
        c.start()

    for s in range(2):
        wait_w(s, 2)
        wait_w(s, 1)
        if s == 0:
            own(s, INNER)
            forward(s)
        else:
            forward(s)
            own(s, INNER)
        wait_own_halo(s)
        own(s, OUTER)
        wait_w(s, 0)
        wait_edges(s)
        earlier_small(s, EDGES)
        finish(s, 0, 7, 2)
        send_edges(s + 1)
        wait_middle(s)
        earlier_small(s, MIDDLE)
        finish(s, 1, 5, 2)
        send_middle(s + 1)
        wait_inner(s)
        earlier(s, INNER)
        finish(s, 2, 1, 4)
        send_inner(s + 1)

    forward(2)
    sum_taps()
    wt_copy.wait()
    wait_own_halo(2)

    def time_product(f, steps, spans):
        parts = []
        for a in steps:
            rows = [X[2, f + a, r : r + n].reshape(n * wide, ch) for r, n in spans]
            parts.append(jnp.concatenate(rows, axis=0))
        lhs = jnp.concatenate(parts, axis=1)
        rhs = jnp.concatenate([wt[a] for a in steps], axis=0)
        return jnp.dot(lhs, rhs, preferred_element_type=F32)

    def double(spans):
        for f, steps in ((0, (0, 1)), (1, (0,))):
            d = time_product(f, steps, spans)
            at = 0
            for r, n in spans:
                v = (d[at : at + n * wide].reshape(n, wide, 2 * ch) + D[f, r : r + n]).astype(BF)
                for j in range(2):
                    U[2 * f + j, r : r + n] = v[:, :, j * ch : (j + 1) * ch]
                at += n * wide

    def space(spans):
        rows_of = [r + k for r, n in spans for k in range(n)]

        def product(unit):
            p, f = unit
            parts = []
            for h in range(2):
                rows = [U[f, r + p + h : r + p + h + n].reshape(n * wide, ch) for r, n in spans]
                parts.append(jnp.concatenate(rows, axis=0))
            lhs = jnp.concatenate(parts, axis=1)
            d = jnp.dot(lhs, wsp[p], preferred_element_type=F32)
            Z[f] = d.reshape(4, wide, 768)

        def spread_columns(unit):
            p, f = unit
            for j, r in enumerate(rows_of):
                z = Z[f, j]
                mid, left, right = z[:, :256], z[:, 256:512], z[:, 512:]
                even = mid - left + shift_down(left)
                odd = mid - right + shift_up(right)
                for h in range(2):
                    T[j, h, pl.ds(0, wide, stride=2), :] = even[:, h * 128 : (h + 1) * 128]
                    T[j, h, pl.ds(1, wide, stride=2), :] = odd[:, h * 128 : (h + 1) * 128]
                out[f, 2 * r + p, :, 0:128] = T[j, 0].astype(BF)
                out[f, 2 * r + p, :, 128:co] = T[j, 1, :, 0 : co - 128].astype(BF)

        units = [(p, f) for p in range(2) for f in range(4)]
        product(units[0])
        for k in range(1, len(units)):
            product(units[k])
            spread_columns(units[k - 1])
        spread_columns(units[-1])

    D[0] = time_product(0, (2,), ((0, 10),)).reshape(10, wide, 2 * ch)
    D[1] = time_product(1, (1, 2), ((0, 10),)).reshape(10, wide, 2 * ch)
    wait_edges(2)
    double(((0, 3), (7, 3)))
    wait_middle(2)
    double(((3, 1), (6, 1)))
    space(OUTER)
    wait_inner(2)
    double(((4, 2),))
    space(INNER)

    for s in range(3):
        @pl.when(has_next)
        def _():
            for k in range(NY):
                y_copy(s, k).wait_send()

        @pl.when(has_up)
        def _():
            t_copy(s, 0).wait_send()

            @pl.when(has_prev)
            def _():
                t_copy(s, 2).wait_send()

        @pl.when(has_down)
        def _():
            t_copy(s, 1).wait_send()

            @pl.when(has_prev)
            def _():
                t_copy(s, 3).wait_send()


def solution(mesh):
    tiles, groups = mesh.shape["tile"], mesh.shape["group"]

    def local(latent, conv_first, conv_second, time_weight, space_weight):
        frames, rows, wide, ch = latent.shape
        co = space_weight.shape[3]
        hbm = pl.BlockSpec(memory_space=pltpu.HBM)
        dma = pltpu.SemaphoreType.DMA
        return pl.pallas_call(
            functools.partial(kernel, tiles, groups),
            name="block",
            out_shape=pltpu.VMEM((2 * frames, 2 * rows, 2 * wide, co), BF),
            in_specs=[hbm] * 5,
            out_specs=pl.BlockSpec(memory_space=pltpu.VMEM),
            scratch_shapes=[
                pltpu.VMEM((2, 8, wide, ch), BF),
                pltpu.VMEM((3, 4, 10, wide, ch), BF),
                pltpu.VMEM((2, 3, 3, 3, ch, ch), BF),
                pltpu.VMEM((3, ch, 2 * ch), BF),
                pltpu.VMEM((3, 3, co, ch), BF),
                pltpu.VMEM((2, 2 * ch, 768), BF),
                pltpu.VMEM((2, 8, wide, 3 * ch), F32),
                pltpu.VMEM((2, 10, wide, 2 * ch), F32),
                pltpu.VMEM((4, 10, wide, ch), BF),
                pltpu.VMEM((4, 4, wide, 768), F32),
                pltpu.VMEM((4, 2, 2 * wide, 128), F32),
                dma,
                dma((2, 3, 3)),
                dma,
                dma,
                dma((3, NY)),
                dma((3, NY)),
                dma((3, 4)),
                dma((3, 4)),
            ],
            compiler_params=pltpu.CompilerParams(
                collective_id=0, has_side_effects=True, vmem_limit_bytes=51 * 2**20
            ),
        )(latent, conv_first, conv_second, time_weight, jnp.swapaxes(space_weight, 2, 3))

    return jax.shard_map(
        local,
        mesh=mesh,
        in_specs=(P("group", "tile", None, None), P(), P(), P(), P()),
        out_specs=P("group", "tile", None, None),
        check_vma=False,
    )
```
